256 devices in a mesh: dp: 8 (over z), space: 32 (over y, x, core).
Axes of the slice: x: 4, y: 4, z: 8, core: 2. Of those that a mesh axis runs over, the one named last changes fastest.
Arguments:
- latents: bfloat16 [8, 256, 256, 320], P('dp', 'space'), may hold values from -14 to 14
- gain_one: float32 [320], replicated, may hold values from 0.1 to 1.9
- shift_one: float32 [320], replicated, may hold values from -2.5 to 2.5
- kernel_one: bfloat16 [3, 3, 320, 320], P(None, None, None, 'dp'), may hold values from -0.109375 to 0.109375
- time_shift: float32 [8, 320], P('dp'), may hold values from -4 to 4
- gain_two: float32 [320], replicated, may hold values from 0.1 to 1.9
- shift_two: float32 [320], replicated, may hold values from -2.5 to 2.5
- kernel_two: bfloat16 [3, 3, 320, 320], P(None, None, None, 'dp'), may hold values from -0.109375 to 0.109375
- bias_two: float32 [320], replicated, may hold values from -2.5 to 2.5
Outputs:
- block_out: bfloat16 [8, 256, 256, 320], P('dp', 'space')
The draws below stay inside these ranges and needn't reach their ends.
All inputs are finite; a program needn't handle non-finite values.
Results may differ from the reference program's by a relative error of at most 0.0041.
Values may be sent and summed in bfloat16 or wider, within the bound.
A program may use at most 128 MiB of HBM per device.

```python
import math
import jax
import jax.numpy as jnp
from jax import lax

C = 320
GROUPS = 32
COLS = 256
HEIGHT = 256
IMAGES = 8


def draw_latents(key, part):
    base_key = jax.random.fold_in(key, 11)
    col_key = jax.random.fold_in(key, 23)
    row_key = jax.random.fold_in(key, 31)
    start_key = jax.random.fold_in(key, 37)
    extent_key = jax.random.fold_in(key, 41)
    loud_key = jax.random.fold_in(key, 43)
    width_group = C // GROUPS
    col_scale = jnp.exp(jax.random.uniform(col_key, (IMAGES, COLS), jnp.float32, 0.0, math.log(3.16)))
    row_scale = jnp.exp(jax.random.uniform(row_key, (IMAGES, HEIGHT, GROUPS), jnp.float32, 0.0, math.log(2.0)))
    start = jax.random.randint(start_key, (IMAGES, GROUPS), 0, HEIGHT)
    low_extent = max(HEIGHT // 16, 1)
    extent = jax.random.randint(extent_key, (IMAGES, GROUPS), low_extent, HEIGHT - low_extent + 1)
    loud = jnp.exp(jax.random.uniform(loud_key, (IMAGES, GROUPS), jnp.float32, math.log(3.0), math.log(12.0)))
    positions = jnp.arange(HEIGHT, dtype=jnp.int32)
    offset = (positions[None, :, None] - start[:, None, :]) % HEIGHT
    inside = offset < extent[:, None, :]
    row_factor = row_scale * jnp.where(inside, loud[:, None, :], 1.0)
    scale = 0.045 * row_factor[:, :, None, :, None] * col_scale[:, None, :, None, None]
    base = jnp.clip(jax.random.normal(base_key, (IMAGES, HEIGHT, COLS, GROUPS, width_group), jnp.float32), -4.0, 4.0)
    return (base * scale).reshape(IMAGES, HEIGHT, COLS, C).astype(jnp.bfloat16)


def steps_of(key, dims, cuts, least, top_value):
    loudness = 1.0
    for position, parts in cuts:
        steps = jax.random.uniform(jax.random.fold_in(jax.random.fold_in(key, 6), position), (parts,), jnp.float32, least / len(cuts), top_value / len(cuts))
        loudness = loudness * jnp.repeat(jnp.exp(steps), dims[position] // parts).reshape((-1,) + (1,) * (len(dims) - 1 - position))
    return loudness


def gaussian(stream_key, shape, scale, limit, cuts=(), kind=jnp.bfloat16):
    values = jax.random.normal(stream_key, shape, jnp.float32) * scale
    if len(cuts) > 0:
        values = steps_of(stream_key, shape, cuts, -0.22, 0.18) * values
    return jnp.clip(values, min=-limit, max=limit).astype(kind)


def setup_inputs(seed: int = 0) -> dict:
    streams_of = jax.random.split(jax.random.key(seed), 10)
    latents = draw_latents(jax.random.fold_in(streams_of[9], 71), 0)
    gain_one = jnp.clip(1.0 + 0.18 * jax.random.normal(streams_of[1], (C,), jnp.float32), 0.1, 1.9)
    shift_one = gaussian(streams_of[2], (C,), 0.5, 2.5, (), jnp.float32)
    kernel_one = gaussian(streams_of[3], (3, 3, C, C), (9 * C) ** -0.5, 0.109375, ((3, 8),))
    time_shift = gaussian(streams_of[4], (IMAGES, C), 1.0, 4.0, ((0, 8),), jnp.float32)
    gain_two = jnp.clip(1.0 + 0.18 * jax.random.normal(streams_of[5], (C,), jnp.float32), 0.1, 1.9)
    shift_two = gaussian(streams_of[6], (C,), 0.5, 2.5, (), jnp.float32)
    kernel_two = gaussian(streams_of[7], (3, 3, C, C), (9 * C) ** -0.5, 0.109375, ((3, 8),))
    bias_two = gaussian(streams_of[8], (C,), 0.5, 2.5, (), jnp.float32)
    return dict(latents=latents, gain_one=gain_one, shift_one=shift_one, kernel_one=kernel_one, time_shift=time_shift, gain_two=gain_two, shift_two=shift_two, kernel_two=kernel_two, bias_two=bias_two)


epsilon = 1e-05

def group_norm(values, gain, shift):
    grouped = values.reshape(values.shape[0], values.shape[1], GROUPS, C // GROUPS)
    mean = lax.optimization_barrier(jnp.mean(grouped, axis=(0, 1, 3)))
    centered = grouped - mean[None, None, :, None]
    var = lax.optimization_barrier(jnp.mean(centered * centered, axis=(0, 1, 3)))
    scaled = centered * lax.rsqrt(var + epsilon)[None, None, :, None]
    return scaled.reshape(values.shape) * gain + shift

def convolve(act, kernel):
    padded = jnp.pad(act, ((1, 1), (1, 1), (0, 0)))
    total = jnp.zeros((HEIGHT * COLS, C), jnp.float32)
    for row_tap in range(3):
        for col_tap in range(3):
            window = padded[row_tap:row_tap + HEIGHT, col_tap:col_tap + COLS, :].reshape(HEIGHT * COLS, C)
            total = total + jnp.dot(window, kernel[row_tap, col_tap], preferred_element_type=jnp.float32)
    return total.reshape(HEIGHT, COLS, C)

def reference(latents, gain_one, shift_one, kernel_one, time_shift, gain_two, shift_two, kernel_two, bias_two):

    def one_image(pair):
        image, embed = pair
        source = image.astype(jnp.float32)
        act_one = jax.nn.silu(group_norm(source, gain_one, shift_one)).astype(jnp.bfloat16)
        hidden = convolve(act_one, kernel_one) + embed
        act_two = jax.nn.silu(group_norm(hidden, gain_two, shift_two)).astype(jnp.bfloat16)
        result = convolve(act_two, kernel_two) + bias_two + source
        return result.astype(jnp.bfloat16)
    return lax.map(one_image, (latents, time_shift))
```

```python
import functools

import jax
import jax.numpy as jnp
from jax import lax
from jax.experimental import pallas as pl
from jax.experimental.pallas import tpu as pltpu
from jax.sharding import PartitionSpec as P

MESH = pl.DeviceIdType.MESH
BF = jnp.bfloat16
F32 = jnp.float32
C = 320
MAIN = 256
LEFT = 64
TILES = 8
EPSILON = 1e-05
NZ = 8
NS = 32
ROWS = 8
COLS = 256
ORDER = (1, 7, 2, 6, 3, 5, 4)


def group_matrix():
    rows = lax.broadcasted_iota(jnp.int32, (384, 384), 0)
    cols = lax.broadcasted_iota(jnp.int32, (384, 384), 1)
    same = ((rows * 6554) >> 16) == ((cols * 6554) >> 16)
    return jnp.where(same, 1.0, 0.0).astype(BF)


def group_sum(vec, gmat):
    hi = vec.astype(BF)
    rest = vec - hi.astype(F32)
    mid = rest.astype(BF)
    low = (rest - mid.astype(F32)).astype(BF)
    lhs = jnp.concatenate([hi, mid, low, jnp.zeros((13, 384), BF)], axis=0)
    out = jnp.dot(lhs, gmat, preferred_element_type=F32)
    return out[0:1] + out[1:2] + out[2:3]


def to_lanes(block):
    return jnp.concatenate([block[0:1], block[1:2], block[2:3]], axis=1)


def to_rows(vec):
    return jnp.concatenate([vec[:, 0:128], vec[:, 128:256], vec[:, 256:384]], axis=0)


def combine(recv, gmat):
    means = recv[:, 0:3, :]
    squares = jnp.sum(recv[:, 3:6, :], axis=0)
    mean = group_sum(to_lanes(jnp.sum(means, axis=0)), gmat) * (1.0 / (NS * 10))
    centered = means - to_rows(mean)[None]
    total = squares + float(ROWS * COLS) * jnp.sum(centered * centered, axis=0)
    var = group_sum(to_lanes(total), gmat) * (1.0 / (10 * NS * ROWS * COLS))
    return mean[:, :C], lax.rsqrt(var + EPSILON)[:, :C]


def put_stats(st_ref, mean, squares):
    st_ref[...] = jnp.zeros((8, 128), F32)
    for first, vec in ((0, mean), (3, squares)):
        st_ref[first : first + 1, :] = vec[:, 0:128]
        st_ref[first + 1 : first + 2, :] = vec[:, 128:256]
        st_ref[first + 2 : first + 3, 0:64] = vec[:, 256:320]


def silu(v):
    half = 0.5 * v
    return half + half * jnp.tanh(half)


def spread(act):
    zero = jnp.zeros((1, C), BF)
    before = jnp.concatenate([zero, act[: COLS - 1]], axis=0)
    after = jnp.concatenate([act[1:], zero], axis=0)
    rest = jnp.concatenate(
        [before[:, MAIN:], act[:, MAIN:], after[:, MAIN:], jnp.zeros((COLS, LEFT), BF)], axis=1
    )
    return before[:, :MAIN], act[:, :MAIN], after[:, :MAIN], rest


def put_spread(a3, row, act):
    for i, part in enumerate(spread(act)):
        a3[row, :, i * 256 : (i + 1) * 256] = part


def kernel(
    lat, g1, b1, k1, ts, g2, b2, k2, bias, out,
    x, a3, hm, hl, hid, kv, gath, wm, wl, gmat, st, recv, hs, hr, ob,
    lsem, osem, hsem, hrsem, ssem, srsem, wsem, wrsem,
):
    z = lax.axis_index("dp")
    s = lax.axis_index("space")
    y, xx, c = s // 8, (s // 2) % 4, s % 2
    part = c * 4 + (y % 2) * 2 + xx % 2

    barrier = pltpu.get_barrier_semaphore()
    for d in range(1, NS):
        pl.semaphore_signal(barrier, inc=1, device_id=(z, (s + d) % NS), device_id_type=MESH)
    for d in range(1, NZ):
        pl.semaphore_signal(barrier, inc=1, device_id=((z + d) % NZ, s), device_id_type=MESH)

    load_x = pltpu.make_async_copy(lat.at[0], x.at[pl.ds(1, ROWS)], lsem.at[0])
    load_k = [pltpu.make_async_copy(k, kv.at[i], lsem.at[1 + i]) for i, k in enumerate((k1, k2))]
    load_k[0].start()
    load_x.start()
    load_k[1].start()
    gmat[...] = group_matrix()

    def remote(src, dst, send, got, device):
        return pltpu.make_async_remote_copy(
            src_ref=src, dst_ref=dst, send_sem=send, recv_sem=got, device_id=device, device_id_type=MESH
        )

    def pack(n):
        for dy in range(3):
            taps = [kv[n, dy, dx].astype(F32).T for dx in range(3)]
            flat = jnp.concatenate(
                [t[:, :MAIN] for t in taps] + [t[:, MAIN:] for t in taps] + [jnp.zeros((40, LEFT), F32)],
                axis=1,
            ).astype(BF)
            for p in range(TILES):
                gath[n, p, z, dy * 40 : dy * 40 + 40, :] = flat[:, p * 128 : (p + 1) * 128]
        for p in range(TILES):
            gath[n, p, z, 120:128, :] = jnp.zeros((8, 128), BF)

    def first(n, d):
        block = gath.at[n, part, z]
        return remote(block, block, wsem.at[n, d], wrsem.at[n, d], ((z + d) % NZ, s))

    def plane(y_step, x_step):
        return ((y + y_step) % 4 * 4 + (xx + x_step) % 4) * 2 + c

    def second(n, d):
        block = gath.at[n, part, (z - d) % NZ]
        sx = 1 if d % 2 == 0 else 3
        sy = 1 if (d // 2) % 2 == 0 else 3
        targets = (plane(0, sx), plane(sx, 0), plane(sy, sx))
        return [
            remote(block, block, wsem.at[n, 8 * (i + 1) + d], wrsem.at[n, 8 * (i + 1) + d], (z, t))
            for i, t in enumerate(targets)
        ]

    def third(n, d):
        block = gath.at[n, pl.ds(c * 4, 4), (z - d) % NZ]
        other = s + 1 - 2 * c
        return remote(block, block, wsem.at[n, 32 + d], wrsem.at[n, 32 + d], (z, other))

    def start_first(n):
        for d in ORDER:
            first(n, d).start()

    def go_second(n, d):
        first(n, d).wait_recv()
        for copy in second(n, d):
            copy.start()

    def go_third(n, d):
        for copy in second(n, d):
            copy.wait_recv()
        third(n, d).start()

    def end_gather(n):
        for d in ORDER:
            third(n, d).wait_recv()

    def drain(n):
        for d in ORDER:
            first(n, d).wait_send()
            for copy in second(n, d):
                copy.wait_send()
            third(n, d).wait_send()

    def arrange(n):
        for o in range(NZ):
            for dy in range(3):
                low = o * 40
                for p in range(TILES):
                    seg = gath[n, p, o, dy * 40 : dy * 40 + 40, :]
                    cols = slice(dy * 1024 + p * 128, dy * 1024 + p * 128 + 128)
                    side = slice(p * 128, p * 128 + 128)
                    if low + 40 <= MAIN:
                        wm[n, low : low + 40, cols] = seg
                    elif low >= MAIN:
                        at = dy * LEFT + low - MAIN
                        wl[n, at : at + 40, side] = seg
                    else:
                        cut = MAIN - low
                        wm[n, low:MAIN, cols] = seg[:cut]
                        wl[n, dy * LEFT : dy * LEFT + 40 - cut, side] = seg[cut:]

    def stat_copy(n, d):
        return remote(st.at[n], recv.at[n, d - 1], ssem.at[n, d], srsem.at[n], (z, (s + d) % NS))

    def send_stats(n):
        for d in range(1, NS):
            stat_copy(n, d).start()
        recv[n, NS - 1] = st[n]

    def wait_stats(n):
        pltpu.make_async_copy(recv.at[n, pl.ds(0, NS - 1)], recv.at[n, pl.ds(0, NS - 1)], srsem.at[n]).wait()

    def nt(a, b):
        return lax.dot_general(a, b, (((1,), (1,)), ((), ())), preferred_element_type=F32)

    def conv_main(n, row, rows):
        lhs = jnp.concatenate([a3[row + d : row + d + rows].reshape(rows * COLS, 1024) for d in range(3)], axis=1)
        hm[row : row + rows] = nt(lhs, wm[n]).reshape(rows, COLS, MAIN)

    def conv_left(n, row, rows):
        hl[row : row + rows] = nt(a3[row : row + rows].reshape(rows * COLS, 1024), wl[n]).reshape(
            rows, COLS, 3 * LEFT
        )

    def conv_row(row):
        side = hl[row, :, 0:64] + hl[row + 1, :, 64:128] + hl[row + 2, :, 128:192]
        return jnp.concatenate([hm[row], side], axis=1)

    load_k[0].wait()
    pack(0)
    load_x.wait()

    def sum_row(i, total):
        return total + jnp.sum(x[1 + i].astype(F32), axis=0, keepdims=True)

    mean = lax.fori_loop(0, ROWS, sum_row, jnp.zeros((1, C), F32)) * (1.0 / (ROWS * COLS))

    def square_row(i, total):
        v = x[1 + i].astype(F32) - mean
        return total + jnp.sum(v * v, axis=0, keepdims=True)

    squares = lax.fori_loop(0, ROWS, square_row, jnp.zeros((1, C), F32))
    put_stats(st.at[0], mean, squares)

    pl.semaphore_wait(barrier, NS - 1 + NZ - 1)
    start_first(0)
    send_stats(0)
    halo = [
        remote(x.at[1], x.at[9], hsem.at[0], hrsem.at[0], (z, (s + NS - 1) % NS)),
        remote(x.at[8], x.at[0], hsem.at[1], hrsem.at[1], (z, (s + 1) % NS)),
    ]
    for copy in halo:
        copy.start()
    load_k[1].wait()
    pack(1)
    go_second(0, 1)
    go_second(0, 7)
    go_second(0, 2)
    go_second(0, 6)
    wait_stats(0)
    mean, inv = combine(recv[0], gmat[...])
    scale, offset = inv * g1[...].reshape(1, C), b1[...].reshape(1, C)

    def act_row(i, carry):
        put_spread(a3, i, silu((x[i].astype(F32) - mean) * scale + offset).astype(BF))
        return carry

    lax.fori_loop(1, 1 + ROWS, act_row, 0)
    go_second(0, 3)
    go_second(0, 5)
    go_third(0, 1)
    go_third(0, 7)
    go_second(0, 4)
    start_first(1)
    go_third(0, 2)
    go_third(0, 6)

    def halo_act(values, edge):
        return jnp.where(s == edge, 0.0, silu((values.astype(F32) - mean) * scale + offset)).astype(BF)

    for copy in halo:
        copy.wait_recv()
    put_spread(a3, 0, halo_act(x[0], 0))
    put_spread(a3, 9, halo_act(x[9], NS - 1))
    go_third(0, 3)
    go_third(0, 5)
    go_third(0, 4)
    end_gather(0)
    arrange(0)

    conv_main(0, 0, 4)
    go_second(1, 1)
    go_second(1, 7)
    conv_main(0, 4, 4)
    for d in ORDER[2:]:
        go_second(1, d)
    conv_left(0, 0, 10)
    shift = ts[...]

    def hidden_sum(i, total):
        side = hl[i, :, 0:64] + hl[i + 1, :, 64:128] + hl[i + 2, :, 128:192]
        v = jnp.concatenate([hm[i], side], axis=1) + shift
        hid[i] = v
        return total + jnp.sum(v, axis=0, keepdims=True)

    mean = lax.fori_loop(0, ROWS, hidden_sum, jnp.zeros((1, C), F32)) * (1.0 / (ROWS * COLS))

    def hidden_square(i, total):
        v = hid[i] - mean
        return total + jnp.sum(v * v, axis=0, keepdims=True)

    squares = lax.fori_loop(0, ROWS, hidden_square, jnp.zeros((1, C), F32))
    put_stats(st.at[1], mean, squares)
    send_stats(1)
    for d in ORDER:
        go_third(1, d)
    end_gather(1)
    arrange(1)
    wait_stats(1)
    mean2, inv2 = combine(recv[1], gmat[...])
    scale2, offset2 = inv2 * g2[...].reshape(1, C), b2[...].reshape(1, C)

    def act_two(i):
        return silu((hid[i] - mean2) * scale2 + offset2).astype(BF)

    sides = []
    for i, (row, step) in enumerate(((0, NS - 1), (ROWS - 1, 1))):
        act = act_two(row)
        hs[i] = act
        copy = remote(hs.at[i], hr.at[1 - i], hsem.at[2 + i], hrsem.at[2 + i], (z, (s + step) % NS))
        copy.start()
        sides.append(copy)
        put_spread(a3, 1 + row, act)

    def act_two_row(i, carry):
        put_spread(a3, 1 + i, act_two(i))
        return carry

    lax.fori_loop(1, ROWS - 1, act_two_row, 0)
    conv_main(1, 1, 6)
    conv_left(1, 1, 8)
    for copy in sides:
        copy.wait_recv()
    zero = jnp.zeros((COLS, C), BF)
    put_spread(a3, 0, jnp.where(s == 0, zero, hr[0]))
    put_spread(a3, 9, jnp.where(s == NS - 1, zero, hr[1]))
    conv_main(1, 0, 1)
    conv_main(1, 7, 1)
    conv_left(1, 0, 1)
    conv_left(1, 9, 1)
    last = bias[...].reshape(1, C)

    def out_row(i, carry):
        side = hl[i, :, 0:64] + hl[i + 1, :, 64:128] + hl[i + 2, :, 128:192]
        v = jnp.concatenate([hm[i], side], axis=1) + last + x[1 + i].astype(F32)
        ob[i] = v.astype(BF)
        return carry

    lax.fori_loop(0, ROWS, out_row, 0)
    store = pltpu.make_async_copy(ob, out.at[0], osem)
    store.start()
    for n in range(2):
        for d in range(1, NS):
            stat_copy(n, d).wait_send()
        drain(n)
    for copy in halo + sides:
        copy.wait_send()
    store.wait()


def local(latents, gain_one, shift_one, kernel_one, time_shift, gain_two, shift_two, kernel_two, bias_two):
    hbm = pl.BlockSpec(memory_space=pl.ANY)
    vmem = pl.BlockSpec(memory_space=pltpu.VMEM)
    return pl.pallas_call(
        kernel,
        out_shape=jax.ShapeDtypeStruct((1, ROWS, COLS, C), BF),
        in_specs=[hbm, vmem, vmem, hbm, vmem, vmem, vmem, hbm, vmem],
        out_specs=hbm,
        scratch_shapes=[
            pltpu.VMEM((10, COLS, C), BF),
            pltpu.VMEM((10, COLS, 1024), BF),
            pltpu.VMEM((ROWS, COLS, MAIN), F32),
            pltpu.VMEM((10, COLS, 3 * LEFT), F32),
            pltpu.VMEM((ROWS, COLS, C), F32),
            pltpu.VMEM((2, 3, 3, C, 40), BF),
            pltpu.VMEM((2, TILES, NZ, 128, 128), BF),
            pltpu.VMEM((2, MAIN, 3072), BF),
            pltpu.VMEM((2, 3 * LEFT, 1024), BF),
            pltpu.VMEM((384, 384), BF),
            pltpu.VMEM((2, 8, 128), F32),
            pltpu.VMEM((2, NS, 8, 128), F32),
            pltpu.VMEM((2, COLS, C), BF),
            pltpu.VMEM((2, COLS, C), BF),
            pltpu.VMEM((ROWS, COLS, C), BF),
            pltpu.SemaphoreType.DMA((3,)),
            pltpu.SemaphoreType.DMA,
            pltpu.SemaphoreType.DMA((4,)),
            pltpu.SemaphoreType.DMA((4,)),
            pltpu.SemaphoreType.DMA((2, NS)),
            pltpu.SemaphoreType.DMA((2,)),
            pltpu.SemaphoreType.DMA((2, 40)),
            pltpu.SemaphoreType.DMA((2, 40)),
        ],
        compiler_params=pltpu.CompilerParams(
            collective_id=0, has_side_effects=True, vmem_limit_bytes=60 * 2**20
        ),
        name="block",
    )(latents, gain_one, shift_one, kernel_one, time_shift, gain_two, shift_two, kernel_two, bias_two)


def solution(mesh):
    return jax.shard_map(
        local,
        mesh=mesh,
        in_specs=(
            P("dp", "space", None, None),
            P(),
            P(),
            P(None, None, None, "dp"),
            P("dp", None),
            P(),
            P(),
            P(None, None, None, "dp"),
            P(),
        ),
        out_specs=P("dp", "space", None, None),
        check_vma=False,
    )
```

```python
import functools

import jax
import jax.numpy as jnp
from jax import lax
from jax.experimental import pallas as pl
from jax.experimental.pallas import tpu as pltpu
from jax.sharding import PartitionSpec as P

MESH = pl.DeviceIdType.MESH
BF = jnp.bfloat16
F32 = jnp.float32
C = 320
MAIN = 256
LEFT = 64
TILES = 8
EPSILON = 1e-05
NZ = 8
NS = 32
ROWS = 8
COLS = 256
ORDER = (1, 7, 2, 6, 3, 5, 4)


def group_matrix():
    rows = lax.broadcasted_iota(jnp.int32, (384, 384), 0)
    cols = lax.broadcasted_iota(jnp.int32, (384, 384), 1)
    same = ((rows * 6554) >> 16) == ((cols * 6554) >> 16)
    return jnp.where(same, 1.0, 0.0).astype(BF)


def group_sum(vec, gmat):
    hi = vec.astype(BF)
    rest = vec - hi.astype(F32)
    mid = rest.astype(BF)
    low = (rest - mid.astype(F32)).astype(BF)
    lhs = jnp.concatenate([hi, mid, low, jnp.zeros((13, 384), BF)], axis=0)
    out = jnp.dot(lhs, gmat, preferred_element_type=F32)
    return out[0:1] + out[1:2] + out[2:3]


def to_lanes(block):
    return jnp.concatenate([block[0:1], block[1:2], block[2:3]], axis=1)


def to_rows(vec):
    return jnp.concatenate([vec[:, 0:128], vec[:, 128:256], vec[:, 256:384]], axis=0)


def combine(recv, gmat, gain, shift):
    means = recv[:, 0:3, :]
    squares = jnp.sum(recv[:, 3:6, :], axis=0)
    mean = group_sum(to_lanes(jnp.sum(means, axis=0)), gmat) * (1.0 / (NS * 10))
    centered = means - to_rows(mean)[None]
    total = squares + float(ROWS * COLS) * jnp.sum(centered * centered, axis=0)
    var = group_sum(to_lanes(total), gmat) * (1.0 / (10 * NS * ROWS * COLS))
    scale = 0.5 * lax.rsqrt(var + EPSILON)[:, :C] * gain
    offset = 0.5 * shift - mean[:, :C] * scale
    return columns(scale), columns(offset)


def columns(vec):
    return jnp.broadcast_to(vec, (128, C)).T


def wide(cols):
    return jnp.concatenate([cols, cols], axis=1)


def fold(v):
    return v[:, :128] + v[:, 128:]


def put_stats(st_ref, base, sums, squares):
    first = base.T[0:1]
    total = jnp.sum(sums.T, axis=0, keepdims=True)
    square = jnp.sum(squares.T, axis=0, keepdims=True)
    shift = total * (1.0 / (ROWS * COLS))
    st_ref[...] = jnp.zeros((8, 128), F32)
    for row, vec in ((0, first + shift), (3, square - total * shift)):
        st_ref[row : row + 1, :] = vec[:, 0:128]
        st_ref[row + 1 : row + 2, :] = vec[:, 128:256]
        st_ref[row + 2 : row + 3, 0:64] = vec[:, 256:320]


def act(v, scale, offset):
    half = v * wide(scale) + wide(offset)
    return (half + half * jnp.tanh(half)).astype(BF)


def taps(a):
    zero = jnp.zeros((a.shape[0], 1), BF)
    return jnp.concatenate([zero, a[:, : COLS - 1]], axis=1), a, jnp.concatenate([a[:, 1:], zero], axis=1)


def put_taps(a3, row, a):
    for i, t in enumerate(taps(a)):
        a3[row, i * MAIN : (i + 1) * MAIN] = t[:MAIN]
        a3[row, 3 * MAIN + i * LEFT : 3 * MAIN + (i + 1) * LEFT] = t[MAIN:]


def kernel(
    lat, g1, b1, k1, ts, g2, b2, k2, bias, out,
    x, a3, hid, kv, gath, w, gmat, par, st, recv, hs, hr, ob,
    lsem, osem, hsem, hrsem, ssem, srsem, wsem, wrsem,
):
    z = lax.axis_index("dp")
    s = lax.axis_index("space")
    y, xx, c = s // 8, (s // 2) % 4, s % 2
    part = c * 4 + (y % 2) * 2 + xx % 2

    barrier = pltpu.get_barrier_semaphore()
    for d in range(1, NS):
        pl.semaphore_signal(barrier, inc=1, device_id=(z, (s + d) % NS), device_id_type=MESH)
    for d in range(1, NZ):
        pl.semaphore_signal(barrier, inc=1, device_id=((z + d) % NZ, s), device_id_type=MESH)

    load_x = pltpu.make_async_copy(lat.at[0], x.at[pl.ds(1, ROWS)], lsem.at[0])
    load_k = [pltpu.make_async_copy(k, kv.at[i], lsem.at[1 + i]) for i, k in enumerate((k1, k2))]
    load_k[0].start()
    load_x.start()
    load_k[1].start()
    gmat[...] = group_matrix()
    for row in range(10):
        a3[row, 960:1024] = jnp.zeros((64, COLS), BF)
    par[0] = columns(ts[...])
    par[1] = columns(bias[...].reshape(1, C))

    def remote(src, dst, send, got, device):
        return pltpu.make_async_remote_copy(
            src_ref=src, dst_ref=dst, send_sem=send, recv_sem=got, device_id=device, device_id_type=MESH
        )

    def pack(n):
        for dy in range(3):
            pieces = [kv[n, dy, dx] for dx in range(3)]
            flat = jnp.concatenate(
                [t[:, :MAIN] for t in pieces] + [t[:, MAIN:] for t in pieces] + [jnp.zeros((40, LEFT), BF)],
                axis=1,
            )
            for p in range(TILES):
                gath[n, p, z, dy * 40 : dy * 40 + 40, :] = flat[:, p * 128 : (p + 1) * 128]
        for p in range(TILES):
            gath[n, p, z, 120:128, :] = jnp.zeros((8, 128), BF)

    def first(n, d):
        block = gath.at[n, part, z]
        return remote(block, block, wsem.at[n, d], wrsem.at[n, d], ((z + d) % NZ, s))

    def plane(y_step, x_step):
        return ((y + y_step) % 4 * 4 + (xx + x_step) % 4) * 2 + c

    def second(n, d):
        block = gath.at[n, part, (z - d) % NZ]
        sx = 1 if d % 2 == 0 else 3
        sy = 1 if (d // 2) % 2 == 0 else 3
        targets = (plane(0, sx), plane(sx, 0), plane(sy, sx))
        return [
            remote(block, block, wsem.at[n, 8 * (i + 1) + d], wrsem.at[n, 8 * (i + 1) + d], (z, t))
            for i, t in enumerate(targets)
        ]

    def third(n, d):
        block = gath.at[n, pl.ds(c * 4, 4), (z - d) % NZ]
        other = s + 1 - 2 * c
        return remote(block, block, wsem.at[n, 32 + d], wrsem.at[n, 32 + d], (z, other))

    def start_first(n):
        for d in ORDER:
            first(n, d).start()

    def go_second(n, d):
        first(n, d).wait_recv()
        for copy in second(n, d):
            copy.start()

    def go_third(n, d):
        for copy in second(n, d):
            copy.wait_recv()
        third(n, d).start()

    def end_gather(n):
        for d in ORDER:
            third(n, d).wait_recv()

    def drain(n):
        for d in ORDER:
            first(n, d).wait_send()
            for copy in second(n, d):
                copy.wait_send()
            third(n, d).wait_send()

    def arrange(n):
        for o in range(NZ):
            for dy in range(3):
                for p in range(TILES):
                    cols = slice(dy * 1024 + p * 128, dy * 1024 + p * 128 + 128)
                    w[n, o * 40 : o * 40 + 40, cols] = gath[n, p, o, dy * 40 : dy * 40 + 40, :]

    def stat_copy(n, d):
        return remote(st.at[n], recv.at[n, d - 1], ssem.at[n, d], srsem.at[n], (z, (s + d) % NS))

    def send_stats(n):
        for d in range(1, NS):
            stat_copy(n, d).start()
        recv[n, NS - 1] = st[n]

    def wait_stats(n):
        pltpu.make_async_copy(recv.at[n, pl.ds(0, NS - 1)], recv.at[n, pl.ds(0, NS - 1)], srsem.at[n]).wait()

    def conv(n, row):
        rhs = jnp.concatenate([a3[row + d] for d in range(3)], axis=0)
        return jnp.dot(w[n], rhs, preferred_element_type=F32)

    load_k[0].wait()
    pack(0)
    load_x.wait()
    base = jnp.broadcast_to(
        jnp.sum(fold(x[1].astype(F32)), axis=1, keepdims=True) * (1.0 / COLS), (C, 128)
    )
    par[2] = base

    def sum_row(i, carry):
        v = x[1 + i].astype(F32) - wide(par[2])
        par[3] += fold(v)
        par[4] += fold(v * v)
        return carry

    par[3] = jnp.zeros((C, 128), F32)
    par[4] = jnp.zeros((C, 128), F32)
    lax.fori_loop(0, ROWS, sum_row, 0)
    put_stats(st.at[0], par[2], par[3], par[4])

    pl.semaphore_wait(barrier, NS - 1 + NZ - 1)
    start_first(0)
    send_stats(0)
    halo = [
        remote(x.at[1], x.at[9], hsem.at[0], hrsem.at[0], (z, (s + NS - 1) % NS)),
        remote(x.at[8], x.at[0], hsem.at[1], hrsem.at[1], (z, (s + 1) % NS)),
    ]
    for copy in halo:
        copy.start()
    load_k[1].wait()
    pack(1)
    go_second(0, 1)
    go_second(0, 7)
    go_second(0, 2)
    go_second(0, 6)
    wait_stats(0)
    par[5], par[6] = combine(recv[0], gmat[...], g1[...].reshape(1, C), b1[...].reshape(1, C))

    def act_block(i, carry):
        low = pl.multiple_of(i * LEFT, LEFT)
        rows = pl.ds(low, LEFT)
        scale, offset = par[5, rows], par[6, rows]
        for row in range(1, 1 + ROWS):
            for k, t in enumerate(taps(act(x[row, rows].astype(F32), scale, offset))):
                at = jnp.where(i < 4, k * MAIN + low, 3 * MAIN + k * LEFT)
                a3[row, pl.ds(pl.multiple_of(at, LEFT), LEFT)] = t
        return carry

    lax.fori_loop(0, 5, act_block, 0)
    go_second(0, 3)
    go_second(0, 5)
    go_third(0, 1)
    go_third(0, 7)
    go_second(0, 4)
    start_first(1)
    go_third(0, 2)
    go_third(0, 6)

    for copy in halo:
        copy.wait_recv()
    for row, edge in ((0, 0), (9, NS - 1)):
        a = act(x[row].astype(F32), par[5], par[6])
        put_taps(a3, row, jnp.where(s == edge, jnp.zeros((C, COLS), BF), a))
    go_third(0, 3)
    go_third(0, 5)
    go_third(0, 4)
    end_gather(0)
    arrange(0)

    for row in range(ROWS):
        v = conv(0, row) + wide(par[0])
        hid[row] = v
        if row == 0:
            base = jnp.broadcast_to(jnp.sum(fold(v), axis=1, keepdims=True) * (1.0 / COLS), (C, 128))
            par[2] = base
            v = v - wide(base)
            par[3] = fold(v)
            par[4] = fold(v * v)
        else:
            v = v - wide(par[2])
            par[3] += fold(v)
            par[4] += fold(v * v)
        if row == 1:
            go_second(1, 1)
            go_second(1, 7)
        if row == 3:
            go_second(1, 2)
            go_second(1, 6)
        if row == 5:
            go_second(1, 3)
            go_second(1, 5)
            go_second(1, 4)
    put_stats(st.at[1], par[2], par[3], par[4])
    send_stats(1)
    for d in ORDER:
        go_third(1, d)
    end_gather(1)
    arrange(1)
    wait_stats(1)
    par[5], par[6] = combine(recv[1], gmat[...], g2[...].reshape(1, C), b2[...].reshape(1, C))

    sides = []
    for i, (row, step) in enumerate(((0, NS - 1), (ROWS - 1, 1))):
        a = act(hid[row], par[5], par[6])
        hs[i] = a
        copy = remote(hs.at[i], hr.at[1 - i], hsem.at[2 + i], hrsem.at[2 + i], (z, (s + step) % NS))
        copy.start()
        sides.append(copy)
        put_taps(a3, 1 + row, a)

    stores = []

    def finish(row):
        v = conv(1, row) + wide(par[1]) + x[1 + row].astype(F32)
        ob[row] = v.astype(BF)
        store = pltpu.make_async_copy(ob.at[row], out.at[0, row], osem.at[row])
        store.start()
        stores.append(store)

    put_taps(a3, 2, act(hid[1], par[5], par[6]))
    for row in range(1, ROWS - 1):
        if row < ROWS - 2:
            put_taps(a3, row + 2, act(hid[row + 1], par[5], par[6]))
        finish(row)
    for copy in sides:
        copy.wait_recv()
    zero = jnp.zeros((C, COLS), BF)
    put_taps(a3, 0, jnp.where(s == 0, zero, hr[0]))
    put_taps(a3, 9, jnp.where(s == NS - 1, zero, hr[1]))
    finish(0)
    finish(ROWS - 1)
    for n in range(2):
        for d in range(1, NS):
            stat_copy(n, d).wait_send()
        drain(n)
    for copy in halo + sides:
        copy.wait_send()
    for store in stores:
        store.wait()


def local(latents, gain_one, shift_one, kernel_one, time_shift, gain_two, shift_two, kernel_two, bias_two):
    hbm = pl.BlockSpec(memory_space=pl.ANY)
    vmem = pl.BlockSpec(memory_space=pltpu.VMEM)
    result = pl.pallas_call(
        kernel,
        out_shape=jax.ShapeDtypeStruct((1, ROWS, C, COLS), BF),
        in_specs=[hbm, vmem, vmem, hbm, vmem, vmem, vmem, hbm, vmem],
        out_specs=hbm,
        scratch_shapes=[
            pltpu.VMEM((10, C, COLS), BF),
            pltpu.VMEM((10, 1024, COLS), BF),
            pltpu.VMEM((ROWS, C, COLS), F32),
            pltpu.VMEM((2, 3, 3, 40, C), BF),
            pltpu.VMEM((2, TILES, NZ, 128, 128), BF),
            pltpu.VMEM((2, C, 3072), BF),
            pltpu.VMEM((384, 384), BF),
            pltpu.VMEM((7, C, 128), F32),
            pltpu.VMEM((2, 8, 128), F32),
            pltpu.VMEM((2, NS, 8, 128), F32),
            pltpu.VMEM((2, C, COLS), BF),
            pltpu.VMEM((2, C, COLS), BF),
            pltpu.VMEM((ROWS, C, COLS), BF),
            pltpu.SemaphoreType.DMA((3,)),
            pltpu.SemaphoreType.DMA((ROWS,)),
            pltpu.SemaphoreType.DMA((4,)),
            pltpu.SemaphoreType.DMA((4,)),
            pltpu.SemaphoreType.DMA((2, NS)),
            pltpu.SemaphoreType.DMA((2,)),
            pltpu.SemaphoreType.DMA((2, 40)),
            pltpu.SemaphoreType.DMA((2, 40)),
        ],
        compiler_params=pltpu.CompilerParams(
            collective_id=0, has_side_effects=True, vmem_limit_bytes=60 * 2**20
        ),
        name="block",
    )(
        latents.transpose(0, 1, 3, 2),
        gain_one,
        shift_one,
        kernel_one.transpose(0, 1, 3, 2),
        time_shift,
        gain_two,
        shift_two,
        kernel_two.transpose(0, 1, 3, 2),
        bias_two,
    )
    return result.transpose(0, 1, 3, 2)


def solution(mesh):
    return jax.shard_map(
        local,
        mesh=mesh,
        in_specs=(
            P("dp", "space", None, None),
            P(),
            P(),
            P(None, None, None, "dp"),
            P("dp", None),
            P(),
            P(),
            P(None, None, None, "dp"),
            P(),
        ),
        out_specs=P("dp", "space", None, None),
        check_vma=False,
    )
```

```python
import functools

import jax
import jax.numpy as jnp
from jax import lax
from jax.experimental import pallas as pl
from jax.experimental.pallas import tpu as pltpu
from jax.sharding import PartitionSpec as P

MESH = pl.DeviceIdType.MESH
BF = jnp.bfloat16
F32 = jnp.float32
C = 320
MAIN = 256
LEFT = 64
TILES = 8
EPSILON = 1e-05
NZ = 8
NS = 32
ROWS = 8
COLS = 256
ORDER = (1, 7, 2, 6, 3, 5, 4)
HOPS = (0, 1, 2, 1)
PEERS = tuple(
    sorted(
        ((dy, dx, dc) for dy in range(4) for dx in range(4) for dc in range(2) if dy + dx + dc > 0),
        key=lambda p: -10 * (HOPS[p[0]] + HOPS[p[1]]) - p[2],
    )
)


def group_matrix():
    rows = lax.broadcasted_iota(jnp.int32, (384, 384), 0)
    cols = lax.broadcasted_iota(jnp.int32, (384, 384), 1)
    same = ((rows * 6554) >> 16) == ((cols * 6554) >> 16)
    return jnp.where(same, 1.0, 0.0).astype(BF)


def group_sum(vec, gmat):
    hi = vec.astype(BF)
    rest = vec - hi.astype(F32)
    mid = rest.astype(BF)
    low = (rest - mid.astype(F32)).astype(BF)
    lhs = jnp.concatenate([hi, mid, low, jnp.zeros((13, 384), BF)], axis=0)
    out = jnp.dot(lhs, gmat, preferred_element_type=F32)
    return out[0:1] + out[1:2] + out[2:3]


def to_lanes(block):
    return jnp.concatenate([block[0:1], block[1:2], block[2:3]], axis=1)


def to_rows(vec):
    return jnp.concatenate([vec[:, 0:128], vec[:, 128:256], vec[:, 256:384]], axis=0)


def combine(recv, gmat, gain, shift):
    means = recv[:, 0:3, :]
    squares = jnp.sum(recv[:, 3:6, :], axis=0)
    mean = group_sum(to_lanes(jnp.sum(means, axis=0)), gmat) * (1.0 / (NS * 10))
    centered = means - to_rows(mean)[None]
    total = squares + float(ROWS * COLS) * jnp.sum(centered * centered, axis=0)
    var = group_sum(to_lanes(total), gmat) * (1.0 / (10 * NS * ROWS * COLS))
    scale = 0.5 * lax.rsqrt(var + EPSILON)[:, :C] * gain
    offset = 0.5 * shift - mean[:, :C] * scale
    return columns(scale), columns(offset)


def columns(vec):
    return jnp.broadcast_to(vec, (128, C)).T


def wide(cols):
    return jnp.concatenate([cols, cols], axis=1)


def fold(v):
    return v[:, :128] + v[:, 128:]


def put_stats(st_ref, base, sums, squares):
    first = base.T[0:1]
    total = jnp.sum(sums.T, axis=0, keepdims=True)
    square = jnp.sum(squares.T, axis=0, keepdims=True)
    shift = total * (1.0 / (ROWS * COLS))
    st_ref[...] = jnp.zeros((8, 128), F32)
    for row, vec in ((0, first + shift), (3, square - total * shift)):
        st_ref[row : row + 1, :] = vec[:, 0:128]
        st_ref[row + 1 : row + 2, :] = vec[:, 128:256]
        st_ref[row + 2 : row + 3, 0:64] = vec[:, 256:320]


def act(v, scale, offset):
    half = v * wide(scale) + wide(offset)
    return (half + half * jnp.tanh(half)).astype(BF)


def taps(a):
    zero = jnp.zeros((a.shape[0], 1), BF)
    return jnp.concatenate([zero, a[:, : COLS - 1]], axis=1), a, jnp.concatenate([a[:, 1:], zero], axis=1)


def put_taps(a3, row, a):
    for i, t in enumerate(taps(a)):
        a3[row, i * MAIN : (i + 1) * MAIN] = t[:MAIN]
        a3[row, 3 * MAIN + i * LEFT : 3 * MAIN + (i + 1) * LEFT] = t[MAIN:]


def kernel(
    lat, g1, b1, k1, ts, g2, b2, k2, bias, out,
    x, a3, hid, kv, gath, w, gmat, par, st, recv, hs, hr,
    lsem, hsem, hrsem, ssem, srsem, wsem, wrsem,
):
    z = lax.axis_index("dp")
    s = lax.axis_index("space")
    y, xx, c = s // 8, (s // 2) % 4, s % 2
    part = c * 4 + (y % 2) * 2 + xx % 2

    barrier = pltpu.get_barrier_semaphore()
    for d in range(1, NS):
        pl.semaphore_signal(barrier, inc=1, device_id=(z, (s + d) % NS), device_id_type=MESH)
    for d in range(1, NZ):
        pl.semaphore_signal(barrier, inc=1, device_id=((z + d) % NZ, s), device_id_type=MESH)

    load_x = pltpu.make_async_copy(lat.at[0], x.at[pl.ds(1, ROWS)], lsem.at[0])
    load_k = [pltpu.make_async_copy(k, kv.at[i], lsem.at[1 + i]) for i, k in enumerate((k1, k2))]
    load_k[0].start()
    load_x.start()
    load_k[1].start()
    gmat[...] = group_matrix()
    for row in range(10):
        a3[row, 960:1024] = jnp.zeros((64, COLS), BF)
    par[0] = columns(ts[...])
    par[1] = columns(bias[...].reshape(1, C))

    def remote(src, dst, send, got, device):
        return pltpu.make_async_remote_copy(
            src_ref=src, dst_ref=dst, send_sem=send, recv_sem=got, device_id=device, device_id_type=MESH
        )

    def pack(n):
        for dy in range(3):
            pieces = [kv[n, dy, dx] for dx in range(3)]
            flat = jnp.concatenate(
                [t[:, :MAIN] for t in pieces] + [t[:, MAIN:] for t in pieces] + [jnp.zeros((40, LEFT), BF)],
                axis=1,
            )
            for p in range(TILES):
                gath[n, p, z, dy * 40 : dy * 40 + 40, :] = flat[:, p * 128 : (p + 1) * 128]
        for p in range(TILES):
            gath[n, p, z, 120:128, :] = jnp.zeros((8, 128), BF)

    def first(n, d):
        block = gath.at[n, part, z]
        return remote(block, block, wsem.at[n, d], wrsem.at[n, d], ((z + d) % NZ, s))

    def plane(y_step, x_step):
        return ((y + y_step) % 4 * 4 + (xx + x_step) % 4) * 2 + c

    def second(n, d):
        block = gath.at[n, part, (z - d) % NZ]
        sx = 1 if d % 2 == 0 else 3
        sy = 1 if (d // 2) % 2 == 0 else 3
        targets = (plane(0, sx), plane(sx, 0), plane(sy, sx))
        return [
            remote(block, block, wsem.at[n, 8 * (i + 1) + d], wrsem.at[n, 8 * (i + 1) + d], (z, t))
            for i, t in enumerate(targets)
        ]

    def third(n, d):
        block = gath.at[n, pl.ds(c * 4, 4), (z - d) % NZ]
        other = s + 1 - 2 * c
        return remote(block, block, wsem.at[n, 32 + d], wrsem.at[n, 32 + d], (z, other))

    def start_first(n):
        for d in ORDER:
            first(n, d).start()

    def go_second(n, d):
        first(n, d).wait_recv()
        for copy in second(n, d):
            copy.start()

    def go_third(n):
        for d in ORDER:
            for copy in second(n, d):
                copy.wait_recv()
            third(n, d).start()

    def end_gather(n):
        for d in ORDER:
            third(n, d).wait_recv()

    def drain(n):
        for d in ORDER:
            first(n, d).wait_send()
            for copy in second(n, d):
                copy.wait_send()
            third(n, d).wait_send()

    def arrange(n, half):
        def tile(q, carry):
            for o in range(NZ):
                for dy in range(3):
                    cols = pl.ds(pl.multiple_of(dy * 512 + q * 128, 128), 128)
                    w[n, half, o * 40 : o * 40 + 40, cols] = gath[n, half * 4 + q, o, dy * 40 : dy * 40 + 40, :]
            return carry

        lax.fori_loop(0, 4, tile, 0)

    def stat_copy(n, d):
        dy, dx, dc = PEERS[d - 1]
        peer = ((y + dy) % 4 * 4 + (xx + dx) % 4) * 2 + (c + dc) % 2
        return remote(st.at[n], recv.at[n, d - 1], ssem.at[n, d], srsem.at[n], (z, peer))

    def send_stats(n):
        for d in range(1, NS):
            stat_copy(n, d).start()
        recv[n, NS - 1] = st[n]

    def wait_stats(n):
        pltpu.make_async_copy(recv.at[n, pl.ds(0, NS - 1)], recv.at[n, pl.ds(0, NS - 1)], srsem.at[n]).wait()

    def conv_half(row, half):
        rows = pl.ds(pl.multiple_of(half * 512, 512), 512)
        rhs = jnp.concatenate([a3[row + d, rows] for d in range(3)], axis=0)
        return jnp.dot(w[0, half], rhs, preferred_element_type=F32)

    def conv_two(row):
        rhs = jnp.concatenate([a3[row + d, h * 512 : h * 512 + 512] for h in range(2) for d in range(3)], axis=0)
        return jnp.dot(jnp.concatenate([w[1, 0], w[1, 1]], axis=1), rhs, preferred_element_type=F32)

    load_k[0].wait()
    pack(0)
    load_x.wait()
    base = jnp.broadcast_to(
        jnp.sum(fold(x[1].astype(F32)), axis=1, keepdims=True) * (1.0 / COLS), (C, 128)
    )
    par[2] = base

    def sum_row(i, carry):
        v = x[1 + i].astype(F32) - wide(par[2])
        par[3] += fold(v)
        par[4] += fold(v * v)
        return carry

    par[3] = jnp.zeros((C, 128), F32)
    par[4] = jnp.zeros((C, 128), F32)
    lax.fori_loop(0, ROWS, sum_row, 0)
    put_stats(st.at[0], par[2], par[3], par[4])

    pl.semaphore_wait(barrier, NS - 1 + NZ - 1)
    start_first(0)
    send_stats(0)
    halo = [
        remote(x.at[1], x.at[9], hsem.at[0], hrsem.at[0], (z, (s + NS - 1) % NS)),
        remote(x.at[8], x.at[0], hsem.at[1], hrsem.at[1], (z, (s + 1) % NS)),
    ]
    for copy in halo:
        copy.start()
    load_k[1].wait()
    pack(1)
    go_second(0, 1)
    go_second(0, 7)
    go_second(0, 2)
    go_second(0, 6)
    wait_stats(0)
    par[5], par[6] = combine(recv[0], gmat[...], g1[...].reshape(1, C), b1[...].reshape(1, C))

    def act_block(i, carry):
        low = pl.multiple_of(i * LEFT, LEFT)
        rows = pl.ds(low, LEFT)
        scale, offset = par[5, rows], par[6, rows]
        for row in range(1, 1 + ROWS):
            for k, t in enumerate(taps(act(x[row, rows].astype(F32), scale, offset))):
                at = jnp.where(i < 4, k * MAIN + low, 3 * MAIN + k * LEFT)
                a3[row, pl.ds(pl.multiple_of(at, LEFT), LEFT)] = t
        return carry

    lax.fori_loop(0, 5, act_block, 0)
    go_second(0, 3)
    go_second(0, 5)
    go_second(0, 4)
    start_first(1)
    for copy in halo:
        copy.wait_recv()
    for row, edge in ((0, 0), (9, NS - 1)):
        a = act(x[row].astype(F32), par[5], par[6])
        put_taps(a3, row, jnp.where(s == edge, jnp.zeros((C, COLS), BF), a))
    go_third(0)
    arrange(0, c)
    for row in range(ROWS):
        hid[row] = conv_half(row, c)
        if row == 5:
            go_second(1, 1)
            go_second(1, 7)
    end_gather(0)
    arrange(0, 1 - c)
    for row in range(ROWS):
        v = hid[row] + conv_half(row, 1 - c) + wide(par[0])
        hid[row] = v
        if row == 0:
            base = jnp.broadcast_to(jnp.sum(fold(v), axis=1, keepdims=True) * (1.0 / COLS), (C, 128))
            par[2] = base
            v = v - wide(base)
            par[3] = fold(v)
            par[4] = fold(v * v)
        else:
            v = v - wide(par[2])
            par[3] += fold(v)
            par[4] += fold(v * v)
        if row == 1:
            go_second(1, 2)
            go_second(1, 6)
        if row == 4:
            go_second(1, 3)
            go_second(1, 5)
        if row == 6:
            go_second(1, 4)
    put_stats(st.at[1], par[2], par[3], par[4])
    send_stats(1)
    go_third(1)
    arrange(1, c)
    wait_stats(1)
    par[5], par[6] = combine(recv[1], gmat[...], g2[...].reshape(1, C), b2[...].reshape(1, C))

    sides = []
    for i, (row, step) in enumerate(((0, NS - 1), (ROWS - 1, 1))):
        a = act(hid[row], par[5], par[6])
        hs[i] = a
        copy = remote(hs.at[i], hr.at[1 - i], hsem.at[2 + i], hrsem.at[2 + i], (z, (s + step) % NS))
        copy.start()
        sides.append(copy)
        put_taps(a3, 1 + row, a)
    end_gather(1)
    arrange(1, 1 - c)

    def finish(row):
        v = conv_two(row) + wide(par[1]) + x[1 + row].astype(F32)
        out[0, row] = v.astype(BF)

    put_taps(a3, 2, act(hid[1], par[5], par[6]))
    for row in range(1, ROWS - 1):
        if row < ROWS - 2:
            put_taps(a3, row + 2, act(hid[row + 1], par[5], par[6]))
        finish(row)
    for copy in sides:
        copy.wait_recv()
    zero = jnp.zeros((C, COLS), BF)
    put_taps(a3, 0, jnp.where(s == 0, zero, hr[0]))
    put_taps(a3, 9, jnp.where(s == NS - 1, zero, hr[1]))
    finish(0)
    finish(ROWS - 1)
    for n in range(2):
        for d in range(1, NS):
            stat_copy(n, d).wait_send()
        drain(n)
    for copy in halo + sides:
        copy.wait_send()


def local(latents, gain_one, shift_one, kernel_one, time_shift, gain_two, shift_two, kernel_two, bias_two):
    hbm = pl.BlockSpec(memory_space=pl.ANY)
    vmem = pl.BlockSpec(memory_space=pltpu.VMEM)
    result = pl.pallas_call(
        kernel,
        out_shape=pltpu.VMEM((1, ROWS, C, COLS), BF),
        in_specs=[hbm, vmem, vmem, hbm, vmem, vmem, vmem, hbm, vmem],
        out_specs=vmem,
        scratch_shapes=[
            pltpu.VMEM((10, C, COLS), BF),
            pltpu.VMEM((10, 1024, COLS), BF),
            pltpu.VMEM((ROWS, C, COLS), F32),
            pltpu.VMEM((2, 3, 3, 40, C), BF),
            pltpu.VMEM((2, TILES, NZ, 128, 128), BF),
            pltpu.VMEM((2, 2, C, 1536), BF),
            pltpu.VMEM((384, 384), BF),
            pltpu.VMEM((7, C, 128), F32),
            pltpu.VMEM((2, 8, 128), F32),
            pltpu.VMEM((2, NS, 8, 128), F32),
            pltpu.VMEM((2, C, COLS), BF),
            pltpu.VMEM((2, C, COLS), BF),
            pltpu.SemaphoreType.DMA((3,)),
            pltpu.SemaphoreType.DMA((4,)),
            pltpu.SemaphoreType.DMA((4,)),
            pltpu.SemaphoreType.DMA((2, NS)),
            pltpu.SemaphoreType.DMA((2,)),
            pltpu.SemaphoreType.DMA((2, 40)),
            pltpu.SemaphoreType.DMA((2, 40)),
        ],
        compiler_params=pltpu.CompilerParams(
            collective_id=0, has_side_effects=True, vmem_limit_bytes=60 * 2**20
        ),
        name="block",
    )(
        latents.transpose(0, 1, 3, 2),
        gain_one,
        shift_one,
        kernel_one.transpose(0, 1, 3, 2),
        time_shift,
        gain_two,
        shift_two,
        kernel_two.transpose(0, 1, 3, 2),
        bias_two,
    )
    return result.transpose(0, 1, 3, 2)


def solution(mesh):
    return jax.shard_map(
        local,
        mesh=mesh,
        in_specs=(
            P("dp", "space", None, None),
            P(),
            P(),
            P(None, None, None, "dp"),
            P("dp", None),
            P(),
            P(),
            P(None, None, None, "dp"),
            P(),
        ),
        out_specs=P("dp", "space", None, None),
        check_vma=False,
    )
```

```python
import functools

import jax
import jax.numpy as jnp
from jax import lax
from jax.experimental import pallas as pl
from jax.experimental.pallas import tpu as pltpu
from jax.sharding import PartitionSpec as P

MESH = pl.DeviceIdType.MESH
BF = jnp.bfloat16
F32 = jnp.float32
C = 320
MAIN = 256
LEFT = 64
TILES = 8
EPSILON = 1e-05
NZ = 8
NS = 32
ROWS = 8
COLS = 256
ORDER = (1, 7, 2, 6, 3, 5, 4)
HOPS = (0, 1, 2, 1)
PEERS = tuple(
    sorted(
        ((dy, dx, dc) for dy in range(4) for dx in range(4) for dc in range(2) if dy + dx + dc > 0),
        key=lambda p: -10 * (HOPS[p[0]] + HOPS[p[1]]) - p[2],
    )
)


def group_matrix():
    rows = lax.broadcasted_iota(jnp.int32, (384, 384), 0)
    cols = lax.broadcasted_iota(jnp.int32, (384, 384), 1)
    same = ((rows * 6554) >> 16) == ((cols * 6554) >> 16)
    return jnp.where(same, 1.0, 0.0).astype(BF)


def group_sum(vec, gmat):
    hi = vec.astype(BF)
    rest = vec - hi.astype(F32)
    mid = rest.astype(BF)
    low = (rest - mid.astype(F32)).astype(BF)
    lhs = jnp.concatenate([hi, mid, low, jnp.zeros((13, 384), BF)], axis=0)
    out = jnp.dot(lhs, gmat, preferred_element_type=F32)
    return out[0:1] + out[1:2] + out[2:3]


def to_lanes(block):
    return jnp.concatenate([block[0:1], block[1:2], block[2:3]], axis=1)


def to_rows(vec):
    return jnp.concatenate([vec[:, 0:128], vec[:, 128:256], vec[:, 256:384]], axis=0)


def combine(recv, gmat, gain, shift):
    means = recv[:, 0:3, :]
    squares = jnp.sum(recv[:, 3:6, :], axis=0)
    mean = group_sum(to_lanes(jnp.sum(means, axis=0)), gmat) * (1.0 / (NS * 10))
    centered = means - to_rows(mean)[None]
    total = squares + float(ROWS * COLS) * jnp.sum(centered * centered, axis=0)
    var = group_sum(to_lanes(total), gmat) * (1.0 / (10 * NS * ROWS * COLS))
    scale = 0.5 * lax.rsqrt(var + EPSILON)[:, :C] * gain
    offset = 0.5 * shift - mean[:, :C] * scale
    return columns(scale), columns(offset)


def columns(vec):
    return jnp.broadcast_to(vec, (128, C)).T


def wide(cols):
    return jnp.concatenate([cols, cols], axis=1)


def fold(v):
    return v[:, :128] + v[:, 128:]


def put_stats(st_ref, base, sums, squares):
    first = base.T[0:1]
    total = jnp.sum(sums.T, axis=0, keepdims=True)
    square = jnp.sum(squares.T, axis=0, keepdims=True)
    shift = total * (1.0 / (ROWS * COLS))
    st_ref[...] = jnp.zeros((8, 128), F32)
    for row, vec in ((0, first + shift), (3, square - total * shift)):
        st_ref[row : row + 1, :] = vec[:, 0:128]
        st_ref[row + 1 : row + 2, :] = vec[:, 128:256]
        st_ref[row + 2 : row + 3, 0:64] = vec[:, 256:320]


def act(v, scale, offset):
    half = v * wide(scale) + wide(offset)
    return (half + half * jnp.tanh(half)).astype(BF)


def taps(a):
    zero = jnp.zeros((a.shape[0], 1), BF)
    return jnp.concatenate([zero, a[:, : COLS - 1]], axis=1), a, jnp.concatenate([a[:, 1:], zero], axis=1)


def put_taps(a3, row, a):
    for i, t in enumerate(taps(a)):
        a3[row, i * MAIN : (i + 1) * MAIN] = t[:MAIN]
        a3[row, 3 * MAIN + i * LEFT : 3 * MAIN + (i + 1) * LEFT] = t[MAIN:]


def kernel(
    lat, g1, b1, k1, ts, g2, b2, k2, bias, out,
    x, a3, hid, kv, gath, w, gmat, par, st, recv, hs, hr,
    lsem, hsem, hrsem, ssem, srsem, wsem, wrsem,
):
    z = lax.axis_index("dp")
    s = lax.axis_index("space")
    y, xx, c = s // 8, (s // 2) % 4, s % 2
    part = c * 4 + (y % 2) * 2 + xx % 2

    barrier = pltpu.get_barrier_semaphore()
    for d in range(1, NS):
        pl.semaphore_signal(barrier, inc=1, device_id=(z, (s + d) % NS), device_id_type=MESH)
    for d in range(1, NZ):
        pl.semaphore_signal(barrier, inc=1, device_id=((z + d) % NZ, s), device_id_type=MESH)

    load_x = pltpu.make_async_copy(lat.at[0], x.at[pl.ds(1, ROWS)], lsem.at[0])
    load_k = [pltpu.make_async_copy(k, kv.at[i], lsem.at[1 + i]) for i, k in enumerate((k1, k2))]
    load_k[0].start()
    load_x.start()
    load_k[1].start()
    gmat[...] = group_matrix()
    for row in range(10):
        a3[row, 960:1024] = jnp.zeros((64, COLS), BF)
    par[0] = columns(ts[...])
    par[1] = columns(bias[...].reshape(1, C))

    def remote(src, dst, send, got, device):
        return pltpu.make_async_remote_copy(
            src_ref=src, dst_ref=dst, send_sem=send, recv_sem=got, device_id=device, device_id_type=MESH
        )

    def pack(n):
        for dy in range(3):
            pieces = [kv[n, dy, dx] for dx in range(3)]
            flat = jnp.concatenate(
                [t[:, :MAIN] for t in pieces] + [t[:, MAIN:] for t in pieces] + [jnp.zeros((40, LEFT), BF)],
                axis=1,
            )
            for p in range(TILES):
                gath[n, p, z, dy * 40 : dy * 40 + 40, :] = flat[:, p * 128 : (p + 1) * 128]
        for p in range(TILES):
            gath[n, p, z, 120:128, :] = jnp.zeros((8, 128), BF)

    def first(n, d):
        block = gath.at[n, part, z]
        return remote(block, block, wsem.at[n, d], wrsem.at[n, d], ((z + d) % NZ, s))

    def plane(y_step, x_step):
        return ((y + y_step) % 4 * 4 + (xx + x_step) % 4) * 2 + c

    def second(n, d):
        block = gath.at[n, part, (z - d) % NZ]
        sx = 1 if d % 2 == 0 else 3
        sy = 1 if (d // 2) % 2 == 0 else 3
        targets = (plane(0, sx), plane(sx, 0), plane(sy, sx))
        return [
            remote(block, block, wsem.at[n, 8 * (i + 1) + d], wrsem.at[n, 8 * (i + 1) + d], (z, t))
            for i, t in enumerate(targets)
        ]

    def third(n, d):
        block = gath.at[n, pl.ds(c * 4, 4), (z - d) % NZ]
        other = s + 1 - 2 * c
        return remote(block, block, wsem.at[n, 32 + d], wrsem.at[n, 32 + d], (z, other))

    def start_first(n):
        for d in ORDER:
            first(n, d).start()

    def go_second(n, d):
        first(n, d).wait_recv()
        for copy in second(n, d):
            copy.start()

    def go_third(n):
        for d in ORDER:
            for copy in second(n, d):
                copy.wait_recv()
            third(n, d).start()

    def end_gather(n):
        for d in ORDER:
            third(n, d).wait_recv()

    def drain(n):
        for d in ORDER:
            first(n, d).wait_send()
            for copy in second(n, d):
                copy.wait_send()
            third(n, d).wait_send()

    def arrange(n, half):
        def tile(q, carry):
            for o in range(NZ):
                for dy in range(3):
                    cols = pl.ds(pl.multiple_of(dy * 512 + q * 128, 128), 128)
                    w[n, half, o * 40 : o * 40 + 40, cols] = gath[n, half * 4 + q, o, dy * 40 : dy * 40 + 40, :]
            return carry

        lax.fori_loop(0, 4, tile, 0)

    def stat_copy(n, d):
        dy, dx, dc = PEERS[d - 1]
        peer = ((y + dy) % 4 * 4 + (xx + dx) % 4) * 2 + (c + dc) % 2
        return remote(st.at[n], recv.at[n, d - 1], ssem.at[n, d], srsem.at[n], (z, peer))

    def send_stats(n):
        for d in range(1, NS):
            stat_copy(n, d).start()
        recv[n, NS - 1] = st[n]

    def wait_stats(n):
        pltpu.make_async_copy(recv.at[n, pl.ds(0, NS - 1)], recv.at[n, pl.ds(0, NS - 1)], srsem.at[n]).wait()

    def conv_half(row, half):
        rows = pl.ds(pl.multiple_of(half * 512, 512), 512)
        rhs = jnp.concatenate([a3[row + d, rows] for d in range(3)], axis=0)
        return jnp.dot(w[0, half], rhs, preferred_element_type=F32)

    def conv_two(row):
        rhs = jnp.concatenate([a3[row + d, h * 512 : h * 512 + 512] for h in range(2) for d in range(3)], axis=0)
        return jnp.dot(jnp.concatenate([w[1, 0], w[1, 1]], axis=1), rhs, preferred_element_type=F32)

    load_k[0].wait()
    pack(0)
    load_x.wait()
    base = jnp.broadcast_to(
        jnp.sum(fold(x[1].astype(F32)), axis=1, keepdims=True) * (1.0 / COLS), (C, 128)
    )
    par[2] = base

    def sum_row(i, carry):
        v = x[1 + i].astype(F32) - wide(par[2])
        par[3] += fold(v)
        par[4] += fold(v * v)
        return carry

    par[3] = jnp.zeros((C, 128), F32)
    par[4] = jnp.zeros((C, 128), F32)
    lax.fori_loop(0, ROWS, sum_row, 0)
    put_stats(st.at[0], par[2], par[3], par[4])

    pl.semaphore_wait(barrier, NS - 1 + NZ - 1)
    start_first(0)
    send_stats(0)
    halo = [
        remote(x.at[1], x.at[9], hsem.at[0], hrsem.at[0], (z, (s + NS - 1) % NS)),
        remote(x.at[8], x.at[0], hsem.at[1], hrsem.at[1], (z, (s + 1) % NS)),
    ]
    for copy in halo:
        copy.start()
    load_k[1].wait()
    pack(1)
    go_second(0, 1)
    go_second(0, 7)
    go_second(0, 2)
    go_second(0, 6)
    wait_stats(0)
    par[5], par[6] = combine(recv[0], gmat[...], g1[...].reshape(1, C), b1[...].reshape(1, C))

    def act_block(i, carry):
        low = pl.multiple_of(i * LEFT, LEFT)
        rows = pl.ds(low, LEFT)
        scale, offset = par[5, rows], par[6, rows]
        for row in range(1, 1 + ROWS):
            for k, t in enumerate(taps(act(x[row, rows].astype(F32), scale, offset))):
                at = jnp.where(i < 4, k * MAIN + low, 3 * MAIN + k * LEFT)
                a3[row, pl.ds(pl.multiple_of(at, LEFT), LEFT)] = t
        return carry

    lax.fori_loop(0, 5, act_block, 0)
    go_second(0, 3)
    go_second(0, 5)
    go_second(0, 4)
    start_first(1)
    for copy in halo:
        copy.wait_recv()
    for row, edge in ((0, 0), (9, NS - 1)):
        a = act(x[row].astype(F32), par[5], par[6])
        put_taps(a3, row, jnp.where(s == edge, jnp.zeros((C, COLS), BF), a))
    go_third(0)
    arrange(0, c)
    for row in range(ROWS):
        hid[row] = conv_half(row, c)
        if row == 5:
            go_second(1, 1)
            go_second(1, 7)
    end_gather(0)
    arrange(0, 1 - c)
    for row in range(ROWS):
        v = hid[row] + conv_half(row, 1 - c) + wide(par[0])
        hid[row] = v
        if row == 0:
            base = jnp.broadcast_to(jnp.sum(fold(v), axis=1, keepdims=True) * (1.0 / COLS), (C, 128))
            par[2] = base
            v = v - wide(base)
            par[3] = fold(v)
            par[4] = fold(v * v)
        else:
            v = v - wide(par[2])
            par[3] += fold(v)
            par[4] += fold(v * v)
        if row == 1:
            go_second(1, 2)
            go_second(1, 6)
        if row == 4:
            go_second(1, 3)
            go_second(1, 5)
        if row == 6:
            go_second(1, 4)
    put_stats(st.at[1], par[2], par[3], par[4])
    send_stats(1)
    go_third(1)
    arrange(1, c)
    for d in range(1, NS):
        stat_copy(0, d).wait_send()
    drain(0)
    for copy in halo:
        copy.wait_send()
    wait_stats(1)
    par[5], par[6] = combine(recv[1], gmat[...], g2[...].reshape(1, C), b2[...].reshape(1, C))

    sides = []
    for i, (row, step) in enumerate(((0, NS - 1), (ROWS - 1, 1))):
        a = act(hid[row], par[5], par[6])
        hs[i] = a
        copy = remote(hs.at[i], hr.at[1 - i], hsem.at[2 + i], hrsem.at[2 + i], (z, (s + step) % NS))
        copy.start()
        sides.append(copy)
        put_taps(a3, 1 + row, a)
    end_gather(1)
    arrange(1, 1 - c)

    def finish(row):
        v = conv_two(row) + wide(par[1]) + x[1 + row].astype(F32)
        out[0, row] = v.astype(BF)

    put_taps(a3, 2, act(hid[1], par[5], par[6]))
    for row in range(1, ROWS - 1):
        if row < ROWS - 2:
            put_taps(a3, row + 2, act(hid[row + 1], par[5], par[6]))
        finish(row)
    for d in range(1, NS):
        stat_copy(1, d).wait_send()
    drain(1)
    for copy in sides:
        copy.wait_recv()
    zero = jnp.zeros((C, COLS), BF)
    put_taps(a3, 0, jnp.where(s == 0, zero, hr[0]))
    put_taps(a3, 9, jnp.where(s == NS - 1, zero, hr[1]))
    finish(0)
    finish(ROWS - 1)
    for copy in sides:
        copy.wait_send()


def local(latents, gain_one, shift_one, kernel_one, time_shift, gain_two, shift_two, kernel_two, bias_two):
    hbm = pl.BlockSpec(memory_space=pl.ANY)
    vmem = pl.BlockSpec(memory_space=pltpu.VMEM)
    result = pl.pallas_call(
        kernel,
        out_shape=pltpu.VMEM((1, ROWS, C, COLS), BF),
        in_specs=[hbm, vmem, vmem, hbm, vmem, vmem, vmem, hbm, vmem],
        out_specs=vmem,
        scratch_shapes=[
            pltpu.VMEM((10, C, COLS), BF),
            pltpu.VMEM((10, 1024, COLS), BF),
            pltpu.VMEM((ROWS, C, COLS), F32),
            pltpu.VMEM((2, 3, 3, 40, C), BF),
            pltpu.VMEM((2, TILES, NZ, 128, 128), BF),
            pltpu.VMEM((2, 2, C, 1536), BF),
            pltpu.VMEM((384, 384), BF),
            pltpu.VMEM((7, C, 128), F32),
            pltpu.VMEM((2, 8, 128), F32),
            pltpu.VMEM((2, NS, 8, 128), F32),
            pltpu.VMEM((2, C, COLS), BF),
            pltpu.VMEM((2, C, COLS), BF),
            pltpu.SemaphoreType.DMA((3,)),
            pltpu.SemaphoreType.DMA((4,)),
            pltpu.SemaphoreType.DMA((4,)),
            pltpu.SemaphoreType.DMA((2, NS)),
            pltpu.SemaphoreType.DMA((2,)),
            pltpu.SemaphoreType.DMA((2, 40)),
            pltpu.SemaphoreType.DMA((2, 40)),
        ],
        compiler_params=pltpu.CompilerParams(
            collective_id=0, has_side_effects=True, vmem_limit_bytes=60 * 2**20
        ),
        name="block",
    )(
        latents.transpose(0, 1, 3, 2),
        gain_one,
        shift_one,
        kernel_one.transpose(0, 1, 3, 2),
        time_shift,
        gain_two,
        shift_two,
        kernel_two.transpose(0, 1, 3, 2),
        bias_two,
    )
    return result.transpose(0, 1, 3, 2)


def solution(mesh):
    return jax.shard_map(
        local,
        mesh=mesh,
        in_specs=(
            P("dp", "space", None, None),
            P(),
            P(),
            P(None, None, None, "dp"),
            P("dp", None),
            P(),
            P(),
            P(None, None, None, "dp"),
            P(),
        ),
        out_specs=P("dp", "space", None, None),
        check_vma=False,
    )
```

```python
import functools

import jax
import jax.numpy as jnp
from jax import lax
from jax.experimental import pallas as pl
from jax.experimental.pallas import tpu as pltpu
from jax.sharding import PartitionSpec as P

MESH = pl.DeviceIdType.MESH
BF = jnp.bfloat16
F32 = jnp.float32
C = 320
MAIN = 256
LEFT = 64
TILES = 8
EPSILON = 1e-05
NZ = 8
NS = 32
ROWS = 8
COLS = 256
ORDER = (1, 7, 2, 6, 3, 5, 4)
HOPS = (0, 1, 2, 1)
PEERS = tuple(
    sorted(
        ((dy, dx, dc) for dy in range(4) for dx in range(4) for dc in range(2) if dy + dx + dc > 0),
        key=lambda p: -10 * (HOPS[p[0]] + HOPS[p[1]]) - p[2],
    )
)


def group_matrix():
    rows = lax.broadcasted_iota(jnp.int32, (384, 384), 0)
    cols = lax.broadcasted_iota(jnp.int32, (384, 384), 1)
    same = ((rows * 6554) >> 16) == ((cols * 6554) >> 16)
    return jnp.where(same, 1.0, 0.0).astype(BF)


def group_sum(vec, gmat):
    hi = vec.astype(BF)
    rest = vec - hi.astype(F32)
    mid = rest.astype(BF)
    low = (rest - mid.astype(F32)).astype(BF)
    lhs = jnp.concatenate([hi, mid, low, jnp.zeros((13, 384), BF)], axis=0)
    out = jnp.dot(lhs, gmat, preferred_element_type=F32)
    return out[0:1] + out[1:2] + out[2:3]


def to_lanes(block):
    return jnp.concatenate([block[0:1], block[1:2], block[2:3]], axis=1)


def to_rows(vec):
    return jnp.concatenate([vec[:, 0:128], vec[:, 128:256], vec[:, 256:384]], axis=0)


def combine(recv, gmat, gain, shift):
    means = recv[:, 0:3, :]
    squares = jnp.sum(recv[:, 3:6, :], axis=0)
    mean = group_sum(to_lanes(jnp.sum(means, axis=0)), gmat) * (1.0 / (NS * 10))
    centered = means - to_rows(mean)[None]
    total = squares + float(ROWS * COLS) * jnp.sum(centered * centered, axis=0)
    var = group_sum(to_lanes(total), gmat) * (1.0 / (10 * NS * ROWS * COLS))
    scale = 0.5 * lax.rsqrt(var + EPSILON)[:, :C] * gain
    offset = 0.5 * shift - mean[:, :C] * scale
    return columns(scale), columns(offset)


def columns(vec):
    return jnp.broadcast_to(vec, (128, C)).T


def wide(cols):
    return jnp.concatenate([cols, cols], axis=1)


def fold(v):
    return v[:, :128] + v[:, 128:]


def put_stats(st_ref, base, sums, squares):
    first = base.T[0:1]
    total = jnp.sum(sums.T, axis=0, keepdims=True)
    square = jnp.sum(squares.T, axis=0, keepdims=True)
    shift = total * (1.0 / (ROWS * COLS))
    st_ref[...] = jnp.zeros((8, 128), F32)
    for row, vec in ((0, first + shift), (3, square - total * shift)):
        st_ref[row : row + 1, :] = vec[:, 0:128]
        st_ref[row + 1 : row + 2, :] = vec[:, 128:256]
        st_ref[row + 2 : row + 3, 0:64] = vec[:, 256:320]


def act(v, scale, offset):
    half = v * wide(scale) + wide(offset)
    return (half + half * jnp.tanh(half)).astype(BF)


def taps(a):
    zero = jnp.zeros((a.shape[0], 1), BF)
    return jnp.concatenate([zero, a[:, : COLS - 1]], axis=1), a, jnp.concatenate([a[:, 1:], zero], axis=1)


def put_taps(a3, row, a):
    for i, t in enumerate(taps(a)):
        a3[row, i * MAIN : (i + 1) * MAIN] = t[:MAIN]
        a3[row, 3 * MAIN + i * LEFT : 3 * MAIN + (i + 1) * LEFT] = t[MAIN:]


def kernel(
    lat, g1, b1, k1, ts, g2, b2, k2, bias, out,
    x, a3, hid, kv, gath, w, gmat, par, st, recv, hs, hr,
    lsem, hsem, hrsem, ssem, srsem, wsem, wrsem,
):
    z = lax.axis_index("dp")
    s = lax.axis_index("space")
    y, xx, c = s // 8, (s // 2) % 4, s % 2
    part = c * 4 + (y % 2) * 2 + xx % 2

    barrier = pltpu.get_barrier_semaphore()
    for d in range(1, NS):
        pl.semaphore_signal(barrier, inc=1, device_id=(z, (s + d) % NS), device_id_type=MESH)
    for d in range(1, NZ):
        pl.semaphore_signal(barrier, inc=1, device_id=((z + d) % NZ, s), device_id_type=MESH)

    load_x = pltpu.make_async_copy(lat.at[0], x.at[pl.ds(1, ROWS)], lsem.at[0])
    load_k = [pltpu.make_async_copy(k, kv.at[i], lsem.at[1 + i]) for i, k in enumerate((k1, k2))]
    load_k[0].start()
    load_x.start()
    load_k[1].start()
    gmat[...] = group_matrix()
    for row in range(10):
        a3[row, 960:1024] = jnp.zeros((64, COLS), BF)
    par[0] = columns(ts[...])
    par[1] = columns(bias[...].reshape(1, C))

    def remote(src, dst, send, got, device):
        return pltpu.make_async_remote_copy(
            src_ref=src, dst_ref=dst, send_sem=send, recv_sem=got, device_id=device, device_id_type=MESH
        )

    def pack(n):
        for dy in range(3):
            pieces = [kv[n, dy, dx] for dx in range(3)]
            flat = jnp.concatenate(
                [t[:, :MAIN] for t in pieces] + [t[:, MAIN:] for t in pieces] + [jnp.zeros((40, LEFT), BF)],
                axis=1,
            )
            for p in range(TILES):
                gath[n, p, z, dy * 40 : dy * 40 + 40, :] = flat[:, p * 128 : (p + 1) * 128]
        for p in range(TILES):
            gath[n, p, z, 120:128, :] = jnp.zeros((8, 128), BF)

    def first(n, d):
        block = gath.at[n, part, z]
        return remote(block, block, wsem.at[n, d], wrsem.at[n, d], ((z + d) % NZ, s))

    def plane(y_step, x_step):
        return ((y + y_step) % 4 * 4 + (xx + x_step) % 4) * 2 + c

    def second(n, d):
        block = gath.at[n, part, (z - d) % NZ]
        sx = 1 if d % 2 == 0 else 3
        sy = 1 if (d // 2) % 2 == 0 else 3
        targets = (plane(0, sx), plane(sx, 0), plane(sy, sx))
        return [
            remote(block, block, wsem.at[n, 8 * (i + 1) + d], wrsem.at[n, 8 * (i + 1) + d], (z, t))
            for i, t in enumerate(targets)
        ]

    def third(n, d):
        block = gath.at[n, pl.ds(c * 4, 4), (z - d) % NZ]
        other = s + 1 - 2 * c
        return remote(block, block, wsem.at[n, 32 + d], wrsem.at[n, 32 + d], (z, other))

    def start_first(n):
        for d in ORDER:
            first(n, d).start()

    def go_second(n, d):
        first(n, d).wait_recv()
        for copy in second(n, d):
            copy.start()

    def go_third(n):
        for d in ORDER:
            for copy in second(n, d):
                copy.wait_recv()
            third(n, d).start()

    def end_gather(n):
        for d in ORDER:
            third(n, d).wait_recv()

    def drain(n):
        for d in ORDER:
            first(n, d).wait_send()
            for copy in second(n, d):
                copy.wait_send()
            third(n, d).wait_send()

    def arrange(n, half):
        def tile(q, carry):
            for o in range(NZ):
                for dy in range(3):
                    cols = pl.ds(pl.multiple_of(dy * 512 + q * 128, 128), 128)
                    w[n, half, o * 40 : o * 40 + 40, cols] = gath[n, half * 4 + q, o, dy * 40 : dy * 40 + 40, :]
            return carry

        lax.fori_loop(0, 4, tile, 0)

    def stat_copy(n, d):
        dy, dx, dc = PEERS[d - 1]
        peer = ((y + dy) % 4 * 4 + (xx + dx) % 4) * 2 + (c + dc) % 2
        return remote(st.at[n], recv.at[n, d - 1], ssem.at[n, d], srsem.at[n], (z, peer))

    def send_stats(n):
        for d in range(1, NS):
            stat_copy(n, d).start()
        recv[n, NS - 1] = st[n]

    def wait_stats(n):
        pltpu.make_async_copy(recv.at[n, pl.ds(0, NS - 1)], recv.at[n, pl.ds(0, NS - 1)], srsem.at[n]).wait()

    def conv_half(row, half):
        rows = pl.ds(pl.multiple_of(half * 512, 512), 512)
        rhs = jnp.concatenate([a3[row + d, rows] for d in range(3)], axis=0)
        return jnp.dot(w[0, half], rhs, preferred_element_type=F32)

    def conv_two(row):
        rhs = jnp.concatenate([a3[row + d, h * 512 : h * 512 + 512] for h in range(2) for d in range(3)], axis=0)
        return jnp.dot(jnp.concatenate([w[1, 0], w[1, 1]], axis=1), rhs, preferred_element_type=F32)

    load_k[0].wait()
    pack(0)
    load_x.wait()
    base = jnp.broadcast_to(
        jnp.sum(fold(x[1].astype(F32)), axis=1, keepdims=True) * (1.0 / COLS), (C, 128)
    )
    par[2] = base

    def sum_row(i, carry):
        v = x[1 + i].astype(F32) - wide(par[2])
        par[3] += fold(v)
        par[4] += fold(v * v)
        return carry

    par[3] = jnp.zeros((C, 128), F32)
    par[4] = jnp.zeros((C, 128), F32)
    lax.fori_loop(0, ROWS, sum_row, 0)
    put_stats(st.at[0], par[2], par[3], par[4])

    pl.semaphore_wait(barrier, NS - 1 + NZ - 1)
    start_first(0)
    send_stats(0)
    halo = [
        remote(x.at[1], x.at[9], hsem.at[0], hrsem.at[0], (z, (s + NS - 1) % NS)),
        remote(x.at[8], x.at[0], hsem.at[1], hrsem.at[1], (z, (s + 1) % NS)),
    ]
    for copy in halo:
        copy.start()
    load_k[1].wait()
    pack(1)
    go_second(0, 1)
    go_second(0, 7)
    go_second(0, 2)
    go_second(0, 6)
    wait_stats(0)
    par[5], par[6] = combine(recv[0], gmat[...], g1[...].reshape(1, C), b1[...].reshape(1, C))

    def act_block(i, carry):
        low = pl.multiple_of(i * LEFT, LEFT)
        rows = pl.ds(low, LEFT)
        scale, offset = par[5, rows], par[6, rows]
        for row in range(1, 1 + ROWS):
            for k, t in enumerate(taps(act(x[row, rows].astype(F32), scale, offset))):
                at = jnp.where(i < 4, k * MAIN + low, 3 * MAIN + k * LEFT)
                a3[row, pl.ds(pl.multiple_of(at, LEFT), LEFT)] = t
        return carry

    lax.fori_loop(0, 5, act_block, 0)
    go_second(0, 3)
    go_second(0, 5)
    go_second(0, 4)
    start_first(1)
    for copy in halo:
        copy.wait_recv()
    for row, edge in ((0, 0), (9, NS - 1)):
        a = act(x[row].astype(F32), par[5], par[6])
        put_taps(a3, row, jnp.where(s == edge, jnp.zeros((C, COLS), BF), a))
    go_third(0)
    arrange(0, c)
    for row in range(ROWS):
        hid[row] = conv_half(row, c)
        if row == 5:
            go_second(1, 1)
            go_second(1, 7)
    end_gather(0)
    arrange(0, 1 - c)
    for row in range(ROWS):
        v = hid[row] + conv_half(row, 1 - c) + wide(par[0])
        hid[row] = v
        if row == 0:
            base = jnp.broadcast_to(jnp.sum(fold(v), axis=1, keepdims=True) * (1.0 / COLS), (C, 128))
            par[2] = base
            v = v - wide(base)
            par[3] = fold(v)
            par[4] = fold(v * v)
        else:
            v = v - wide(par[2])
            par[3] += fold(v)
            par[4] += fold(v * v)
        if row == 1:
            go_second(1, 2)
            go_second(1, 6)
        if row == 4:
            go_second(1, 3)
            go_second(1, 5)
        if row == 6:
            go_second(1, 4)
    put_stats(st.at[1], par[2], par[3], par[4])
    send_stats(1)
    go_third(1)
    arrange(1, c)
    for d in range(1, NS):
        stat_copy(0, d).wait_send()
    drain(0)
    for copy in halo:
        copy.wait_send()
    wait_stats(1)
    par[5], par[6] = combine(recv[1], gmat[...], g2[...].reshape(1, C), b2[...].reshape(1, C))

    sides = []
    for i, (row, step) in enumerate(((0, NS - 1), (ROWS - 1, 1))):
        a = act(hid[row], par[5], par[6])
        hs[i] = a
        copy = remote(hs.at[i], hr.at[1 - i], hsem.at[2 + i], hrsem.at[2 + i], (z, (s + step) % NS))
        copy.start()
        sides.append(copy)
    for i, row in enumerate((0, ROWS - 1)):
        put_taps(a3, 1 + row, hs[i])
    end_gather(1)
    arrange(1, 1 - c)

    def finish(row):
        v = conv_two(row) + wide(par[1]) + x[1 + row].astype(F32)
        out[0, row] = v.astype(BF)

    put_taps(a3, 2, act(hid[1], par[5], par[6]))
    for row in range(1, ROWS - 1):
        if row < ROWS - 2:
            put_taps(a3, row + 2, act(hid[row + 1], par[5], par[6]))
        finish(row)
    for d in range(1, NS):
        stat_copy(1, d).wait_send()
    drain(1)
    for copy in sides:
        copy.wait_recv()
    zero = jnp.zeros((C, COLS), BF)
    put_taps(a3, 0, jnp.where(s == 0, zero, hr[0]))
    put_taps(a3, 9, jnp.where(s == NS - 1, zero, hr[1]))
    finish(0)
    finish(ROWS - 1)
    for copy in sides:
        copy.wait_send()


def local(latents, gain_one, shift_one, kernel_one, time_shift, gain_two, shift_two, kernel_two, bias_two):
    hbm = pl.BlockSpec(memory_space=pl.ANY)
    vmem = pl.BlockSpec(memory_space=pltpu.VMEM)
    result = pl.pallas_call(
        kernel,
        out_shape=pltpu.VMEM((1, ROWS, C, COLS), BF),
        in_specs=[hbm, vmem, vmem, hbm, vmem, vmem, vmem, hbm, vmem],
        out_specs=vmem,
        scratch_shapes=[
            pltpu.VMEM((10, C, COLS), BF),
            pltpu.VMEM((10, 1024, COLS), BF),
            pltpu.VMEM((ROWS, C, COLS), F32),
            pltpu.VMEM((2, 3, 3, 40, C), BF),
            pltpu.VMEM((2, TILES, NZ, 128, 128), BF),
            pltpu.VMEM((2, 2, C, 1536), BF),
            pltpu.VMEM((384, 384), BF),
            pltpu.VMEM((7, C, 128), F32),
            pltpu.VMEM((2, 8, 128), F32),
            pltpu.VMEM((2, NS, 8, 128), F32),
            pltpu.VMEM((2, C, COLS), BF),
            pltpu.VMEM((2, C, COLS), BF),
            pltpu.SemaphoreType.DMA((3,)),
            pltpu.SemaphoreType.DMA((4,)),
            pltpu.SemaphoreType.DMA((4,)),
            pltpu.SemaphoreType.DMA((2, NS)),
            pltpu.SemaphoreType.DMA((2,)),
            pltpu.SemaphoreType.DMA((2, 40)),
            pltpu.SemaphoreType.DMA((2, 40)),
        ],
        compiler_params=pltpu.CompilerParams(
            collective_id=0, has_side_effects=True, vmem_limit_bytes=60 * 2**20
        ),
        name="block",
    )(
        latents.transpose(0, 1, 3, 2),
        gain_one,
        shift_one,
        kernel_one.transpose(0, 1, 3, 2),
        time_shift,
        gain_two,
        shift_two,
        kernel_two.transpose(0, 1, 3, 2),
        bias_two,
    )
    return result.transpose(0, 1, 3, 2)


def solution(mesh):
    return jax.shard_map(
        local,
        mesh=mesh,
        in_specs=(
            P("dp", "space", None, None),
            P(),
            P(),
            P(None, None, None, "dp"),
            P("dp", None),
            P(),
            P(),
            P(None, None, None, "dp"),
            P(),
        ),
        out_specs=P("dp", "space", None, None),
        check_vma=False,
    )
```
